32 devices in a mesh: group: 2 (over x), seq: 16 (over z, y, core).
Axes of the slice: x: 2, y: 2, z: 4, core: 2. Of those that a mesh axis runs over, the one named last changes fastest.
Arguments:
- queries: bfloat16 [3584, 4096], P(('group', 'seq')), parts along dimension 0, may hold values from -8 to 8
- keys: bfloat16 [3584, 4096], P(('group', 'seq')), parts along dimension 0, may hold values from -8 to 8
- values: bfloat16 [3584, 4096], P(('group', 'seq')), parts along dimension 0, may hold values from -6 to 6
- destination: int32 [3584], P(('group', 'seq')), parts along dimension 0, may hold values from 0 to 1791, as said below
Outputs:
- regrouped: bfloat16 [3584, 4096], P(('group', 'seq')), parts along dimension 0
The draws below stay inside these ranges and needn't reach their ends.
There are 2 independent parts, one for each index of `group`. The reference program is written for one: setup_inputs(seed, part) draws one part's arguments, and reference() takes and returns one part's arrays. A program takes and returns all parts, laid end to end along the dimension named above; each array names one. Nothing has to cross between parts.
Inputs may be any that keep to these rules, and one draw needn't show every extreme that they name: A permutation of the 1792 rows. Of the 112 rows of one device, at most 7 have their destination among the rows of any one device, and some pair of devices reaches 7.
All inputs are finite; a program needn't handle non-finite values.
Results may differ from the reference program's by a relative error of at most 0.0026.
Values may be sent and summed in bfloat16 or wider, within the bound.
A program may use at most 64 MiB of HBM per device.

```python
import math
import jax
import jax.numpy as jnp
from jax import lax

HEADS = 32
HEAD_DIM = 128
TOK_DEV = 112
TOKENS = 1792
N_SEQ = 16


def draw_queries(key, part):
    key = jax.random.fold_in(key, 1)
    array_shape = (TOKENS, HEADS * HEAD_DIM)
    drawn = 2.0 * jax.random.truncated_normal(key, -4.0, 4.0, array_shape, jnp.float32)
    return drawn.astype(jnp.bfloat16)


def draw_keys(key, part):
    key = jax.random.fold_in(key, 2)
    array_shape = (TOKENS, HEADS * HEAD_DIM)
    drawn = 2.0 * jax.random.truncated_normal(key, -4.0, 4.0, array_shape, jnp.float32)
    return drawn.astype(jnp.bfloat16)


def draw_destination(key, part):
    key = jax.random.fold_in(key, 11)
    shift_key, order_key, spot_key = jax.random.split(key, 3)
    devices = N_SEQ
    tok_rows = TOK_DEV
    base_count = tok_rows // devices
    extra_count = tok_rows % devices
    shift = jax.random.randint(shift_key, (), 0, devices)
    source = jnp.arange(devices)[:, None]
    target = jnp.arange(devices)[None, :]
    counts = base_count + ((target - source - shift) % devices < extra_count).astype(jnp.int32)
    running = jnp.cumsum(counts, axis=1)
    block_start = running - counts
    arrive_start = jnp.cumsum(counts, axis=0) - counts
    listed = jnp.arange(tok_rows)[None, :, None]
    dest_list = jnp.sum((running[:, None, :] <= listed).astype(jnp.int32), axis=2)
    order_keys = jax.random.split(order_key, devices)
    local_order = jax.vmap(lambda each: jax.random.permutation(each, tok_rows))(order_keys)
    chosen = jnp.take_along_axis(dest_list, local_order, axis=1)
    start_here = jnp.take_along_axis(block_start, chosen, axis=1)
    arrive_here = arrive_start[jnp.arange(devices)[:, None], chosen]
    position = arrive_here + local_order - start_here
    spot_keys = jax.random.split(spot_key, devices)
    spot_order = jax.vmap(lambda each: jax.random.permutation(each, tok_rows))(spot_keys)
    final_spot = spot_order[chosen, position]
    return (chosen * tok_rows + final_spot).reshape(devices * tok_rows).astype(jnp.int32)


def block_scale(key, extent, cuts, low, largest):
    def one(axis_at, shards_of):
        heights = jax.random.uniform(jax.random.fold_in(jax.random.fold_in(key, 6), axis_at), (shards_of,), jnp.float32, low / len(cuts), largest / len(cuts))
        return jnp.repeat(jnp.exp(heights), extent[axis_at] // shards_of).reshape((-1,) + (1,) * (len(extent) - axis_at - 1))

    factor_of = one(*cuts[0])
    for cut in cuts[1:]:
        factor_of = factor_of * one(*cut)
    return factor_of


def bell_draw(stream_key, extent, spread, most, cuts=(), kind=jnp.bfloat16):
    values = spread * jax.random.normal(stream_key, extent, jnp.float32)
    if cuts:
        values = values * block_scale(stream_key, extent, cuts, -0.22, 0.18)
    return jnp.clip(values, -most, most).astype(kind)


def setup_inputs(seed: int = 0, part: int = 0) -> dict:
    seeds = jax.random.split(jax.random.key(seed), 5)
    part_keys = jax.random.split(jax.random.fold_in(seeds[4], part), 5)
    return {
        "queries": draw_queries(jax.random.fold_in(jax.random.fold_in(seeds[4], part), 71), part),
        "keys": draw_keys(jax.random.fold_in(jax.random.fold_in(seeds[4], part), 71), part),
        "values": bell_draw(part_keys[2], (TOKENS, HEADS * HEAD_DIM), 1.0, 6.0, ((0, 16),)),
        "destination": draw_destination(jax.random.fold_in(jax.random.fold_in(seeds[4], part), 71), part),
    }


def attend_head(query_rows, key_rows, value_rows):
    query_count = query_rows.shape[0]
    block_rows = math.gcd(query_count, 256)
    score_scale = 1.0 / math.sqrt(query_rows.shape[1])

    def one_block(query_block):
        scores = jnp.dot(query_block, key_rows.T, preferred_element_type=jnp.float32) * score_scale
        row_peak = lax.optimization_barrier(jnp.max(scores, axis=1, keepdims=True))
        exp_scores = jnp.exp(scores - row_peak)
        row_total = lax.optimization_barrier(jnp.sum(exp_scores, axis=1))
        weights = exp_scores.astype(jnp.bfloat16)
        mixed = jnp.dot(weights, value_rows, preferred_element_type=jnp.float32)
        return (mixed / row_total[:, None]).astype(jnp.bfloat16)
    blocks = query_rows.reshape(query_count // block_rows, block_rows, query_rows.shape[1])
    return lax.map(one_block, blocks).reshape(query_count, query_rows.shape[1])

def reference(queries, keys, values, destination):
    token_count = queries.shape[0]

    def per_head(head_index):
        column_start = (head_index * HEAD_DIM).astype(jnp.int32)
        query_cols = lax.dynamic_slice_in_dim(queries, column_start, HEAD_DIM, 1)
        key_cols = lax.dynamic_slice_in_dim(keys, column_start, HEAD_DIM, 1)
        value_cols = lax.dynamic_slice_in_dim(values, column_start, HEAD_DIM, 1)
        return attend_head(query_cols, key_cols, value_cols)
    outputs = lax.map(per_head, jnp.arange(HEADS, dtype=jnp.int32))
    attended = jnp.transpose(outputs, (1, 0, 2)).reshape(token_count, HEADS * HEAD_DIM)
    return jnp.zeros_like(attended).at[destination.astype(jnp.int32)].set(attended)
```

```python
import functools
import math

import jax
import jax.numpy as jnp
from jax import lax
from jax.experimental import pallas as pl
from jax.experimental.pallas import tpu as pltpu
from jax.sharding import PartitionSpec as P

HEADS = 32
HEAD_DIM = 128
LANES = 128


def attend_local(query_rows, key_rows, value_rows):
    query_count = query_rows.shape[0]
    block_rows = math.gcd(query_count, 256)
    score_scale = 1.0 / math.sqrt(query_rows.shape[2])

    def one_block(query_block):
        scores = (
            jnp.einsum("qud,kud->uqk", query_block, key_rows, preferred_element_type=jnp.float32)
            * score_scale
        )
        row_peak = jnp.max(scores, axis=2, keepdims=True)
        exp_scores = jnp.exp(scores - row_peak)
        row_total = jnp.sum(exp_scores, axis=2)
        weights = exp_scores.astype(jnp.bfloat16)
        mixed = jnp.einsum("uqk,kud->qud", weights, value_rows, preferred_element_type=jnp.float32)
        return (mixed / jnp.transpose(row_total)[:, :, None]).astype(jnp.bfloat16)

    blocks = query_rows.reshape(
        query_count // block_rows, block_rows, query_rows.shape[1], query_rows.shape[2]
    )
    return lax.map(one_block, blocks).reshape(query_rows.shape)


def regroup_rows(latent_rows, destination, devices):
    tok_rows, features = latent_rows.shape
    capacity = -(-tok_rows // devices)
    target = destination // tok_rows
    dest_pos = destination % tok_rows
    member = (target[:, None] == jnp.arange(devices)[None, :]).astype(jnp.int32)
    before = jnp.sum((jnp.cumsum(member, axis=0) - member) * member, axis=1)
    slot_index = target * capacity + before
    select = jnp.arange(devices * capacity)[:, None] == slot_index[None, :]
    packed = jnp.dot(
        select.astype(jnp.bfloat16), latent_rows, preferred_element_type=jnp.float32
    ).astype(jnp.bfloat16)
    filled = jnp.any(select, axis=1)
    where_to = jnp.where(filled, jnp.sum(jnp.where(select, dest_pos[None, :], 0), axis=1), -1)
    packed = packed.reshape(devices, capacity, features)
    where_to = where_to.reshape(devices, capacity)
    arrived, positions = (
        lax.all_to_all(packed, "seq", split_axis=0, concat_axis=0, tiled=True),
        lax.all_to_all(where_to, "seq", split_axis=0, concat_axis=0, tiled=True),
    )
    picker = (jnp.arange(tok_rows)[:, None] == positions.reshape(1, devices * capacity)).astype(
        jnp.bfloat16
    )
    return jnp.dot(
        picker, arrived.reshape(devices * capacity, features), preferred_element_type=jnp.float32
    ).astype(jnp.bfloat16)


def local(queries, keys, values, destination):
    devices = lax.axis_size("seq")
    tok_rows = queries.shape[0]
    splits = max(1, devices // HEADS)
    per_device = max(1, HEADS // devices)
    part_rows = tok_rows // splits
    head_groups = HEADS // per_device
    shaped = queries.reshape(splits, part_rows, head_groups, per_device, HEAD_DIM)
    query_slots = jnp.transpose(shaped, (1, 2, 0, 3, 4)).reshape(
        part_rows, devices, per_device, HEAD_DIM
    )
    paired_cols = jnp.concatenate(
        (keys.reshape(tok_rows, HEADS, HEAD_DIM), values.reshape(tok_rows, HEADS, HEAD_DIM)), axis=2
    )
    pair_slots = jnp.repeat(
        paired_cols.reshape(tok_rows, head_groups, per_device, 2 * HEAD_DIM), splits, axis=1
    )
    query_heads, pair_heads = (
        lax.all_to_all(query_slots, "seq", split_axis=1, concat_axis=0, tiled=True),
        lax.all_to_all(pair_slots, "seq", split_axis=1, concat_axis=0, tiled=True),
    )
    query_heads = query_heads.reshape(-1, per_device, HEAD_DIM)
    pair_heads = pair_heads.reshape(-1, per_device, 2 * HEAD_DIM)
    attended = attend_local(query_heads, pair_heads[:, :, :HEAD_DIM], pair_heads[:, :, HEAD_DIM:])
    returned = lax.all_to_all(
        attended.reshape(devices, part_rows, per_device, HEAD_DIM),
        "seq",
        split_axis=0,
        concat_axis=0,
        tiled=True,
    )
    returned = returned.reshape(head_groups, splits, part_rows, per_device, HEAD_DIM)
    latent_rows = jnp.transpose(returned, (1, 2, 0, 3, 4)).reshape(tok_rows, HEADS * HEAD_DIM)
    return regroup_rows(latent_rows, destination, devices)


def start_to(me, target, source, landing, send_sem, recv_sem):
    @pl.when(target != me)
    def _():
        pltpu.make_async_remote_copy(
            src_ref=source,
            dst_ref=landing,
            send_sem=send_sem,
            recv_sem=recv_sem,
            device_id={"seq": target},
            device_id_type=pl.DeviceIdType.MESH,
        ).start()

    @pl.when(target == me)
    def _():
        pltpu.make_async_copy(source, landing, recv_sem).start()


def wait_bytes(ref, sem):
    pltpu.make_async_copy(ref, ref, sem).wait()


def attend_kernel(
    devices, heads, q_ref, k_ref, v_ref, spot_ref, out_ref,
    held, spots, spot_row, chosen, moved, mixed,
    spot_send, spot_recv, in_send, in_recv, out_send, out_recv,
):
    me = lax.axis_index("seq")
    rows = q_ref.shape[0]
    tokens = devices * rows
    width = heads * HEAD_DIM
    half = devices // 2
    block = 2 * rows
    factor = math.log2(math.e) / math.sqrt(HEAD_DIM)

    def columns(device, head):
        return pl.ds(pl.multiple_of(device * width + head * HEAD_DIM, LANES), HEAD_DIM)

    def token_rows(device):
        return pl.ds(pl.multiple_of(device * rows, 16), rows)

    barrier = pltpu.get_barrier_semaphore()

    def greet(step, carry):
        pl.semaphore_signal(
            barrier, inc=1, device_id={"seq": lax.rem(me + step, devices)},
            device_id_type=pl.DeviceIdType.MESH,
        )
        return carry

    lax.fori_loop(1, devices, greet, 0)
    pl.semaphore_wait(barrier, devices - 1)

    def send_spots(step, carry):
        target = lax.rem(me + half + step, devices)
        start_to(me, target, spot_ref, spots.at[me], spot_send, spot_recv)
        return carry

    lax.fori_loop(0, devices, send_spots, 0)

    for head in range(heads):
        for kind, whole in enumerate((q_ref, k_ref, v_ref)):

            def send_rows(step, carry):
                target = lax.rem(me + half + step, devices)
                start_to(
                    me, target, whole.at[:, columns(target, head)],
                    held.at[kind, head, token_rows(me)],
                    in_send.at[kind, head], in_recv.at[kind, head],
                )
                return carry

            lax.fori_loop(0, devices, send_rows, 0)

    wait_bytes(spots, spot_recv)
    for device in range(devices):
        spot_row[:, device * rows : (device + 1) * rows] = spots[device, :, :rows]

    def choose(at, carry):
        start = pl.multiple_of(at * block, 16)
        places = lax.broadcasted_iota(jnp.int32, (block, tokens), 0) + start
        chosen[pl.ds(start, block), :] = jnp.where(
            spot_row[0:1, :] == places, 1.0, 0.0
        ).astype(jnp.bfloat16)
        return carry

    lax.fori_loop(0, devices // 2, choose, 0)

    for head in range(heads):
        wait_bytes(held.at[0, head], in_recv.at[0, head])

        def move(at, carry):
            here = pl.ds(pl.multiple_of(at * block, 16), block)
            moved[head, here, :] = jnp.dot(
                chosen[here, :], held[0, head], preferred_element_type=jnp.float32
            ).astype(jnp.bfloat16)
            return carry

        lax.fori_loop(0, devices // 2, move, 0)
        wait_bytes(held.at[1, head], in_recv.at[1, head])
        wait_bytes(held.at[2, head], in_recv.at[2, head])

        def attend(step, carry):
            off = half // 2 + ((step + 1) // 2) * (1 - 2 * lax.rem(step, 2))
            at = lax.rem(me // 2 + off, half)
            here = pl.ds(pl.multiple_of(at * block, 16), block)
            scores = lax.dot_general(
                moved[head, here, :], held[1, head], (((1,), (1,)), ((), ())),
                preferred_element_type=jnp.float32,
            )
            peak = jnp.max(scores, axis=1, keepdims=True)
            grown = jnp.exp2((scores - peak) * factor)
            total = jnp.sum(grown, axis=1, keepdims=True)
            result = jnp.dot(
                grown.astype(jnp.bfloat16), held[2, head], preferred_element_type=jnp.float32
            )
            mixed[head, here, :] = (result / total).astype(jnp.bfloat16)
            for one in range(2):
                target = 2 * at + one
                start_to(
                    me, target, mixed.at[head, token_rows(target)],
                    out_ref.at[:, columns(me, head)], out_send, out_recv,
                )
            return carry

        lax.fori_loop(0, half, attend, 0)

    others = pl.ds(0, (devices - 1) * rows)
    wait_bytes(spots.at[pl.ds(0, devices - 1)], spot_send)
    for head in range(heads):
        for kind in range(3):
            wait_bytes(held.at[kind, head, others], in_send.at[kind, head])
    wait_bytes(mixed.at[:, others], out_send)
    wait_bytes(mixed, out_recv)


def local_fused(queries, keys, values, destination):
    devices = lax.axis_size("seq")
    rows = queries.shape[0]
    heads = HEADS // devices
    tokens = devices * rows
    lanes = -(-rows // LANES) * LANES
    spots = jnp.broadcast_to(
        jnp.pad(destination, (0, lanes - rows), constant_values=-1)[None, :], (8, lanes)
    )
    any_space = pl.BlockSpec(memory_space=pl.ANY)
    return pl.pallas_call(
        functools.partial(attend_kernel, devices, heads),
        out_shape=jax.ShapeDtypeStruct(queries.shape, jnp.bfloat16),
        in_specs=[any_space, any_space, any_space, pl.BlockSpec(memory_space=pltpu.VMEM)],
        out_specs=any_space,
        scratch_shapes=[
            pltpu.VMEM((3, heads, tokens, HEAD_DIM), jnp.bfloat16),
            pltpu.VMEM((devices, 8, lanes), jnp.int32),
            pltpu.VMEM((8, tokens), jnp.int32),
            pltpu.VMEM((tokens, tokens), jnp.bfloat16),
            pltpu.VMEM((heads, tokens, HEAD_DIM), jnp.bfloat16),
            pltpu.VMEM((heads, tokens, HEAD_DIM), jnp.bfloat16),
            pltpu.SemaphoreType.DMA,
            pltpu.SemaphoreType.DMA,
            pltpu.SemaphoreType.DMA((3, heads)),
            pltpu.SemaphoreType.DMA((3, heads)),
            pltpu.SemaphoreType.DMA,
            pltpu.SemaphoreType.DMA,
        ],
        compiler_params=pltpu.CompilerParams(
            collective_id=0, has_side_effects=True, vmem_limit_bytes=48 * 2**20
        ),
        name="attend",
    )(queries, keys, values, spots)


def solution(mesh):
    devices = mesh.shape["seq"]
    fused = HEADS % devices == 0 and devices % 4 == 0
    return jax.shard_map(
        local_fused if fused else local,
        mesh=mesh,
        in_specs=(
            P(("group", "seq"), None),
            P(("group", "seq"), None),
            P(("group", "seq"), None),
            P(("group", "seq")),
        ),
        out_specs=P(("group", "seq"), None),
        check_vma=False,
    )
```

```python
import functools
import math

import jax
import jax.numpy as jnp
from jax import lax
from jax.experimental import pallas as pl
from jax.experimental.pallas import tpu as pltpu
from jax.sharding import PartitionSpec as P

HEADS = 32
HEAD_DIM = 128
LANES = 128


def attend_local(query_rows, key_rows, value_rows):
    query_count = query_rows.shape[0]
    block_rows = math.gcd(query_count, 256)
    score_scale = 1.0 / math.sqrt(query_rows.shape[2])

    def one_block(query_block):
        scores = (
            jnp.einsum("qud,kud->uqk", query_block, key_rows, preferred_element_type=jnp.float32)
            * score_scale
        )
        row_peak = jnp.max(scores, axis=2, keepdims=True)
        exp_scores = jnp.exp(scores - row_peak)
        row_total = jnp.sum(exp_scores, axis=2)
        weights = exp_scores.astype(jnp.bfloat16)
        mixed = jnp.einsum("uqk,kud->qud", weights, value_rows, preferred_element_type=jnp.float32)
        return (mixed / jnp.transpose(row_total)[:, :, None]).astype(jnp.bfloat16)

    blocks = query_rows.reshape(
        query_count // block_rows, block_rows, query_rows.shape[1], query_rows.shape[2]
    )
    return lax.map(one_block, blocks).reshape(query_rows.shape)


def regroup_rows(latent_rows, destination, devices):
    tok_rows, features = latent_rows.shape
    capacity = -(-tok_rows // devices)
    target = destination // tok_rows
    dest_pos = destination % tok_rows
    member = (target[:, None] == jnp.arange(devices)[None, :]).astype(jnp.int32)
    before = jnp.sum((jnp.cumsum(member, axis=0) - member) * member, axis=1)
    slot_index = target * capacity + before
    select = jnp.arange(devices * capacity)[:, None] == slot_index[None, :]
    packed = jnp.dot(
        select.astype(jnp.bfloat16), latent_rows, preferred_element_type=jnp.float32
    ).astype(jnp.bfloat16)
    filled = jnp.any(select, axis=1)
    where_to = jnp.where(filled, jnp.sum(jnp.where(select, dest_pos[None, :], 0), axis=1), -1)
    packed = packed.reshape(devices, capacity, features)
    where_to = where_to.reshape(devices, capacity)
    arrived, positions = (
        lax.all_to_all(packed, "seq", split_axis=0, concat_axis=0, tiled=True),
        lax.all_to_all(where_to, "seq", split_axis=0, concat_axis=0, tiled=True),
    )
    picker = (jnp.arange(tok_rows)[:, None] == positions.reshape(1, devices * capacity)).astype(
        jnp.bfloat16
    )
    return jnp.dot(
        picker, arrived.reshape(devices * capacity, features), preferred_element_type=jnp.float32
    ).astype(jnp.bfloat16)


def local(queries, keys, values, destination):
    devices = lax.axis_size("seq")
    tok_rows = queries.shape[0]
    splits = max(1, devices // HEADS)
    per_device = max(1, HEADS // devices)
    part_rows = tok_rows // splits
    head_groups = HEADS // per_device
    shaped = queries.reshape(splits, part_rows, head_groups, per_device, HEAD_DIM)
    query_slots = jnp.transpose(shaped, (1, 2, 0, 3, 4)).reshape(
        part_rows, devices, per_device, HEAD_DIM
    )
    paired_cols = jnp.concatenate(
        (keys.reshape(tok_rows, HEADS, HEAD_DIM), values.reshape(tok_rows, HEADS, HEAD_DIM)), axis=2
    )
    pair_slots = jnp.repeat(
        paired_cols.reshape(tok_rows, head_groups, per_device, 2 * HEAD_DIM), splits, axis=1
    )
    query_heads, pair_heads = (
        lax.all_to_all(query_slots, "seq", split_axis=1, concat_axis=0, tiled=True),
        lax.all_to_all(pair_slots, "seq", split_axis=1, concat_axis=0, tiled=True),
    )
    query_heads = query_heads.reshape(-1, per_device, HEAD_DIM)
    pair_heads = pair_heads.reshape(-1, per_device, 2 * HEAD_DIM)
    attended = attend_local(query_heads, pair_heads[:, :, :HEAD_DIM], pair_heads[:, :, HEAD_DIM:])
    returned = lax.all_to_all(
        attended.reshape(devices, part_rows, per_device, HEAD_DIM),
        "seq",
        split_axis=0,
        concat_axis=0,
        tiled=True,
    )
    returned = returned.reshape(head_groups, splits, part_rows, per_device, HEAD_DIM)
    latent_rows = jnp.transpose(returned, (1, 2, 0, 3, 4)).reshape(tok_rows, HEADS * HEAD_DIM)
    return regroup_rows(latent_rows, destination, devices)


def start_to(me, target, source, landing, send_sem, recv_sem):
    @pl.when(target != me)
    def _():
        pltpu.make_async_remote_copy(
            src_ref=source,
            dst_ref=landing,
            send_sem=send_sem,
            recv_sem=recv_sem,
            device_id={"seq": target},
            device_id_type=pl.DeviceIdType.MESH,
        ).start()

    @pl.when(target == me)
    def _():
        pltpu.make_async_copy(source, landing, recv_sem).start()


def wait_bytes(ref, sem):
    pltpu.make_async_copy(ref, ref, sem).wait()


def attend_kernel(
    devices, heads, q_ref, k_ref, v_ref, spot_ref, out_ref,
    held, spots, spot_row, chosen, moved, weights, totals, mixed,
    spot_send, spot_recv, in_send, in_recv, out_send, out_recv,
):
    me = lax.axis_index("seq")
    rows = q_ref.shape[0]
    tokens = devices * rows
    width = heads * HEAD_DIM
    half = devices // 2
    block = 2 * rows
    factor = math.log2(math.e) / math.sqrt(HEAD_DIM)

    def columns(device, head):
        return pl.ds(pl.multiple_of(device * width + head * HEAD_DIM, LANES), HEAD_DIM)

    def token_rows(device):
        return pl.ds(pl.multiple_of(device * rows, 16), rows)

    barrier = pltpu.get_barrier_semaphore()

    def greet(step, carry):
        pl.semaphore_signal(
            barrier, inc=1, device_id={"seq": lax.rem(me + step, devices)},
            device_id_type=pl.DeviceIdType.MESH,
        )
        return carry

    lax.fori_loop(1, devices, greet, 0)
    pl.semaphore_wait(barrier, devices - 1)

    def send_spots(step, carry):
        target = lax.rem(me + half + step, devices)
        start_to(me, target, spot_ref, spots.at[me], spot_send, spot_recv)
        return carry

    for head in range(heads):
        for kind, whole in enumerate((q_ref, k_ref, v_ref)):

            def send_rows(step, carry):
                target = lax.rem(me + half + step, devices)
                start_to(
                    me, target, whole.at[:, columns(target, head)],
                    held.at[kind, head, token_rows(me)],
                    in_send.at[kind, head], in_recv.at[kind, head],
                )
                return carry

            lax.fori_loop(0, devices, send_rows, 0)
            if head == 0 and kind == 0:
                lax.fori_loop(0, devices, send_spots, 0)

    wait_bytes(spots, spot_recv)
    for device in range(devices):
        spot_row[:, device * rows : (device + 1) * rows] = spots[device]

    def choose(at, carry):
        start = pl.multiple_of(at * block, 16)
        places = lax.broadcasted_iota(jnp.int32, (block, tokens), 0) + start
        chosen[pl.ds(start, block), :] = jnp.where(
            spot_row[...] == places, 1.0, 0.0
        ).astype(jnp.bfloat16)
        return carry

    lax.fori_loop(0, devices // 2, choose, 0)

    for head in range(heads):
        wait_bytes(held.at[0, head], in_recv.at[0, head])

        def move(at, carry):
            here = pl.ds(pl.multiple_of(at * block, 16), block)
            moved[head, here, :] = jnp.dot(
                chosen[here, :], held[0, head], preferred_element_type=jnp.float32
            ).astype(jnp.bfloat16)
            return carry

        lax.fori_loop(0, devices // 2, move, 0)
        wait_bytes(held.at[1, head], in_recv.at[1, head])

        def weigh(at, carry):
            here = pl.ds(pl.multiple_of(at * block, 16), block)
            scores = lax.dot_general(
                moved[head, here, :], held[1, head], (((1,), (1,)), ((), ())),
                preferred_element_type=jnp.float32,
            )
            peak = jnp.max(scores, axis=1, keepdims=True)
            grown = jnp.exp2((scores - peak) * factor)
            totals[here, :] = jnp.sum(grown, axis=1, keepdims=True)
            weights[here, :] = grown.astype(jnp.bfloat16)
            return carry

        lax.fori_loop(0, half, weigh, 0)
        wait_bytes(held.at[2, head], in_recv.at[2, head])

        def attend(step, carry):
            off = half // 2 + ((step + 1) // 2) * (1 - 2 * lax.rem(step, 2))
            at = lax.rem(me // 2 + off, half)
            here = pl.ds(pl.multiple_of(at * block, 16), block)
            result = jnp.dot(
                weights[here, :], held[2, head], preferred_element_type=jnp.float32
            )
            mixed[head, here, :] = (result / totals[here, :]).astype(jnp.bfloat16)
            for one in range(2):
                target = 2 * at + one
                start_to(
                    me, target, mixed.at[head, token_rows(target)],
                    out_ref.at[:, columns(me, head)], out_send, out_recv,
                )
            return carry

        lax.fori_loop(0, half, attend, 0)

    others = pl.ds(0, (devices - 1) * rows)
    wait_bytes(spots.at[pl.ds(0, devices - 1)], spot_send)
    for head in range(heads):
        for kind in range(3):
            wait_bytes(held.at[kind, head, others], in_send.at[kind, head])
    wait_bytes(mixed.at[:, others], out_send)
    wait_bytes(mixed, out_recv)


def local_fused(queries, keys, values, destination):
    devices = lax.axis_size("seq")
    rows = queries.shape[0]
    heads = HEADS // devices
    tokens = devices * rows
    spots = destination.reshape(1, rows)
    large = pl.BlockSpec(memory_space=pltpu.HBM)
    return pl.pallas_call(
        functools.partial(attend_kernel, devices, heads),
        out_shape=jax.ShapeDtypeStruct(queries.shape, jnp.bfloat16),
        in_specs=[large, large, large, pl.BlockSpec(memory_space=pltpu.VMEM)],
        out_specs=pl.BlockSpec(memory_space=pl.ANY),
        scratch_shapes=[
            pltpu.VMEM((3, heads, tokens, HEAD_DIM), jnp.bfloat16),
            pltpu.VMEM((devices, 1, rows), jnp.int32),
            pltpu.VMEM((1, tokens), jnp.int32),
            pltpu.VMEM((tokens, tokens), jnp.bfloat16),
            pltpu.VMEM((heads, tokens, HEAD_DIM), jnp.bfloat16),
            pltpu.VMEM((tokens, tokens), jnp.bfloat16),
            pltpu.VMEM((tokens, 1), jnp.float32),
            pltpu.VMEM((heads, tokens, HEAD_DIM), jnp.bfloat16),
            pltpu.SemaphoreType.DMA,
            pltpu.SemaphoreType.DMA,
            pltpu.SemaphoreType.DMA((3, heads)),
            pltpu.SemaphoreType.DMA((3, heads)),
            pltpu.SemaphoreType.DMA,
            pltpu.SemaphoreType.DMA,
        ],
        compiler_params=pltpu.CompilerParams(
            collective_id=0, has_side_effects=True, vmem_limit_bytes=60 * 2**20
        ),
        name="attend",
    )(queries, keys, values, spots)


def solution(mesh):
    devices = mesh.shape["seq"]
    fused = HEADS % devices == 0 and devices % 4 == 0
    return jax.shard_map(
        local_fused if fused else local,
        mesh=mesh,
        in_specs=(
            P(("group", "seq"), None),
            P(("group", "seq"), None),
            P(("group", "seq"), None),
            P(("group", "seq")),
        ),
        out_specs=P(("group", "seq"), None),
        check_vma=False,
    )
```

```python
import functools
import math

import jax
import jax.numpy as jnp
from jax import lax
from jax.experimental import pallas as pl
from jax.experimental.pallas import tpu as pltpu
from jax.sharding import PartitionSpec as P

HEADS = 32
HEAD_DIM = 128
LANES = 128


def attend_local(query_rows, key_rows, value_rows):
    query_count = query_rows.shape[0]
    block_rows = math.gcd(query_count, 256)
    score_scale = 1.0 / math.sqrt(query_rows.shape[2])

    def one_block(query_block):
        scores = (
            jnp.einsum("qud,kud->uqk", query_block, key_rows, preferred_element_type=jnp.float32)
            * score_scale
        )
        row_peak = jnp.max(scores, axis=2, keepdims=True)
        exp_scores = jnp.exp(scores - row_peak)
        row_total = jnp.sum(exp_scores, axis=2)
        weights = exp_scores.astype(jnp.bfloat16)
        mixed = jnp.einsum("uqk,kud->qud", weights, value_rows, preferred_element_type=jnp.float32)
        return (mixed / jnp.transpose(row_total)[:, :, None]).astype(jnp.bfloat16)

    blocks = query_rows.reshape(
        query_count // block_rows, block_rows, query_rows.shape[1], query_rows.shape[2]
    )
    return lax.map(one_block, blocks).reshape(query_rows.shape)


def regroup_rows(latent_rows, destination, devices):
    tok_rows, features = latent_rows.shape
    capacity = -(-tok_rows // devices)
    target = destination // tok_rows
    dest_pos = destination % tok_rows
    member = (target[:, None] == jnp.arange(devices)[None, :]).astype(jnp.int32)
    before = jnp.sum((jnp.cumsum(member, axis=0) - member) * member, axis=1)
    slot_index = target * capacity + before
    select = jnp.arange(devices * capacity)[:, None] == slot_index[None, :]
    packed = jnp.dot(
        select.astype(jnp.bfloat16), latent_rows, preferred_element_type=jnp.float32
    ).astype(jnp.bfloat16)
    filled = jnp.any(select, axis=1)
    where_to = jnp.where(filled, jnp.sum(jnp.where(select, dest_pos[None, :], 0), axis=1), -1)
    packed = packed.reshape(devices, capacity, features)
    where_to = where_to.reshape(devices, capacity)
    arrived, positions = (
        lax.all_to_all(packed, "seq", split_axis=0, concat_axis=0, tiled=True),
        lax.all_to_all(where_to, "seq", split_axis=0, concat_axis=0, tiled=True),
    )
    picker = (jnp.arange(tok_rows)[:, None] == positions.reshape(1, devices * capacity)).astype(
        jnp.bfloat16
    )
    return jnp.dot(
        picker, arrived.reshape(devices * capacity, features), preferred_element_type=jnp.float32
    ).astype(jnp.bfloat16)


def local(queries, keys, values, destination):
    devices = lax.axis_size("seq")
    tok_rows = queries.shape[0]
    splits = max(1, devices // HEADS)
    per_device = max(1, HEADS // devices)
    part_rows = tok_rows // splits
    head_groups = HEADS // per_device
    shaped = queries.reshape(splits, part_rows, head_groups, per_device, HEAD_DIM)
    query_slots = jnp.transpose(shaped, (1, 2, 0, 3, 4)).reshape(
        part_rows, devices, per_device, HEAD_DIM
    )
    paired_cols = jnp.concatenate(
        (keys.reshape(tok_rows, HEADS, HEAD_DIM), values.reshape(tok_rows, HEADS, HEAD_DIM)), axis=2
    )
    pair_slots = jnp.repeat(
        paired_cols.reshape(tok_rows, head_groups, per_device, 2 * HEAD_DIM), splits, axis=1
    )
    query_heads, pair_heads = (
        lax.all_to_all(query_slots, "seq", split_axis=1, concat_axis=0, tiled=True),
        lax.all_to_all(pair_slots, "seq", split_axis=1, concat_axis=0, tiled=True),
    )
    query_heads = query_heads.reshape(-1, per_device, HEAD_DIM)
    pair_heads = pair_heads.reshape(-1, per_device, 2 * HEAD_DIM)
    attended = attend_local(query_heads, pair_heads[:, :, :HEAD_DIM], pair_heads[:, :, HEAD_DIM:])
    returned = lax.all_to_all(
        attended.reshape(devices, part_rows, per_device, HEAD_DIM),
        "seq",
        split_axis=0,
        concat_axis=0,
        tiled=True,
    )
    returned = returned.reshape(head_groups, splits, part_rows, per_device, HEAD_DIM)
    latent_rows = jnp.transpose(returned, (1, 2, 0, 3, 4)).reshape(tok_rows, HEADS * HEAD_DIM)
    return regroup_rows(latent_rows, destination, devices)


def start_to(me, target, source, landing, send_sem, recv_sem):
    @pl.when(target != me)
    def _():
        pltpu.make_async_remote_copy(
            src_ref=source,
            dst_ref=landing,
            send_sem=send_sem,
            recv_sem=recv_sem,
            device_id={"seq": target},
            device_id_type=pl.DeviceIdType.MESH,
        ).start()

    @pl.when(target == me)
    def _():
        pltpu.make_async_copy(source, landing, recv_sem).start()


def wait_bytes(ref, sem):
    pltpu.make_async_copy(ref, ref, sem).wait()


def attend_kernel(
    devices, heads, q_ref, k_ref, v_ref, spot_ref, out_ref,
    held, spots, spot_row, chosen, moved, weights, totals, mixed,
    spot_send, spot_recv, in_send, in_recv, out_send, out_recv,
):
    me = lax.axis_index("seq")
    rows = q_ref.shape[0]
    tokens = devices * rows
    width = heads * HEAD_DIM
    half = devices // 2
    block = 2 * rows
    factor = math.log2(math.e) / math.sqrt(HEAD_DIM)

    def columns(device, head):
        return pl.ds(pl.multiple_of(device * width + head * HEAD_DIM, LANES), HEAD_DIM)

    def token_rows(device):
        return pl.ds(pl.multiple_of(device * rows, 16), rows)

    barrier = pltpu.get_barrier_semaphore()

    def greet(step, carry):
        pl.semaphore_signal(
            barrier, inc=1, device_id={"seq": lax.rem(me + step, devices)},
            device_id_type=pl.DeviceIdType.MESH,
        )
        return carry

    lax.fori_loop(1, devices, greet, 0)
    pl.semaphore_wait(barrier, devices - 1)

    def send_spots(step, carry):
        target = lax.rem(me + half + step, devices)
        start_to(me, target, spot_ref, spots.at[me], spot_send, spot_recv)
        return carry

    for head in range(heads):
        for kind, whole in enumerate((q_ref, k_ref, v_ref)):

            def send_rows(step, carry):
                target = lax.rem(me + half + step, devices)
                start_to(
                    me, target, whole.at[:, columns(target, head)],
                    held.at[kind, head, token_rows(me)],
                    in_send.at[kind, head], in_recv.at[kind, head],
                )
                return carry

            lax.fori_loop(0, devices, send_rows, 0)
            if head == 0 and kind == 0:
                lax.fori_loop(0, devices, send_spots, 0)

    wait_bytes(spots, spot_recv)
    for device in range(devices):
        spot_row[:, device * rows : (device + 1) * rows] = spots[device]

    def choose(at, carry):
        start = pl.multiple_of(at * block, 16)
        places = lax.broadcasted_iota(jnp.int32, (block, tokens), 0) + start
        chosen[pl.ds(start, block), :] = jnp.where(
            spot_row[...] == places, 1.0, 0.0
        ).astype(jnp.bfloat16)
        return carry

    lax.fori_loop(0, devices // 2, choose, 0)

    for head in range(heads):
        wait_bytes(held.at[0, head], in_recv.at[0, head])

        def move(at, carry):
            here = pl.ds(pl.multiple_of(at * block, 16), block)
            moved[head, here, :] = jnp.dot(
                chosen[here, :], held[0, head], preferred_element_type=jnp.float32
            ).astype(jnp.bfloat16)
            return carry

        lax.fori_loop(0, devices // 2, move, 0)
        wait_bytes(held.at[1, head], in_recv.at[1, head])

        def weigh(at, carry):
            here = pl.ds(pl.multiple_of(at * block, 16), block)
            scores = lax.dot_general(
                moved[head, here, :], held[1, head], (((1,), (1,)), ((), ())),
                preferred_element_type=jnp.float32,
            )
            peak = jnp.max(scores, axis=1, keepdims=True)
            grown = jnp.exp2((scores - peak) * factor)
            totals[here, :] = jnp.sum(grown, axis=1, keepdims=True)
            weights[here, :] = grown.astype(jnp.bfloat16)
            return carry

        lax.fori_loop(0, half, weigh, 0)
        wait_bytes(held.at[2, head], in_recv.at[2, head])

        def attend(step, carry):
            off = half // 2 + ((step + 1) // 2) * (1 - 2 * lax.rem(step, 2))
            at = lax.rem(me // 2 + off, half)
            here = pl.ds(pl.multiple_of(at * block, 16), block)
            result = jnp.dot(
                weights[here, :], held[2, head], preferred_element_type=jnp.float32
            )
            mixed[head, here, :] = (result / totals[here, :]).astype(jnp.bfloat16)
            for one in range(2):
                target = 2 * at + one
                start_to(
                    me, target, mixed.at[head, token_rows(target)],
                    out_ref.at[:, columns(me, head)], out_send, out_recv,
                )
            return carry

        lax.fori_loop(0, half, attend, 0)

    others = pl.ds(0, (devices - 1) * rows)
    wait_bytes(spots.at[pl.ds(0, devices - 1)], spot_send)
    for head in range(heads):
        for kind in range(3):
            wait_bytes(held.at[kind, head, others], in_send.at[kind, head])
    wait_bytes(mixed.at[:, others], out_send)
    wait_bytes(mixed, out_recv)


def local_fused(queries, keys, values, destination):
    devices = lax.axis_size("seq")
    rows = queries.shape[0]
    heads = HEADS // devices
    tokens = devices * rows
    spots = destination.reshape(1, rows)
    large = pl.BlockSpec(memory_space=pltpu.HBM)
    return pl.pallas_call(
        functools.partial(attend_kernel, devices, heads),
        out_shape=jax.ShapeDtypeStruct(queries.shape, jnp.bfloat16),
        in_specs=[large, large, large, pl.BlockSpec(memory_space=pltpu.VMEM)],
        out_specs=pl.BlockSpec(memory_space=pl.ANY),
        scratch_shapes=[
            pltpu.VMEM((3, heads, tokens, HEAD_DIM), jnp.bfloat16),
            pltpu.VMEM((devices, 1, rows), jnp.int32),
            pltpu.VMEM((1, tokens), jnp.int32),
            pltpu.VMEM((tokens, tokens), jnp.bfloat16),
            pltpu.VMEM((heads, tokens, HEAD_DIM), jnp.bfloat16),
            pltpu.VMEM((tokens, tokens), jnp.bfloat16),
            pltpu.VMEM((tokens, 1), jnp.float32),
            pltpu.VMEM((heads, tokens, HEAD_DIM), jnp.bfloat16),
            pltpu.SemaphoreType.DMA,
            pltpu.SemaphoreType.DMA,
            pltpu.SemaphoreType.DMA((3, heads)),
            pltpu.SemaphoreType.DMA((3, heads)),
            pltpu.SemaphoreType.DMA,
            pltpu.SemaphoreType.DMA,
        ],
        compiler_params=pltpu.CompilerParams(
            collective_id=0, has_side_effects=True, vmem_limit_bytes=53 * 2**20
        ),
        name="attend",
    )(queries, keys, values, spots)


def solution(mesh):
    devices = mesh.shape["seq"]
    fused = HEADS % devices == 0 and devices % 4 == 0
    return jax.shard_map(
        local_fused if fused else local,
        mesh=mesh,
        in_specs=(
            P(("group", "seq"), None),
            P(("group", "seq"), None),
            P(("group", "seq"), None),
            P(("group", "seq")),
        ),
        out_specs=P(("group", "seq"), None),
        check_vma=False,
    )
```

```python
import functools
import math

import jax
import jax.numpy as jnp
from jax import lax
from jax.experimental import pallas as pl
from jax.experimental.pallas import tpu as pltpu
from jax.sharding import PartitionSpec as P

HEADS = 32
HEAD_DIM = 128
LANES = 128


def attend_local(query_rows, key_rows, value_rows):
    query_count = query_rows.shape[0]
    block_rows = math.gcd(query_count, 256)
    score_scale = 1.0 / math.sqrt(query_rows.shape[2])

    def one_block(query_block):
        scores = (
            jnp.einsum("qud,kud->uqk", query_block, key_rows, preferred_element_type=jnp.float32)
            * score_scale
        )
        row_peak = jnp.max(scores, axis=2, keepdims=True)
        exp_scores = jnp.exp(scores - row_peak)
        row_total = jnp.sum(exp_scores, axis=2)
        weights = exp_scores.astype(jnp.bfloat16)
        mixed = jnp.einsum("uqk,kud->qud", weights, value_rows, preferred_element_type=jnp.float32)
        return (mixed / jnp.transpose(row_total)[:, :, None]).astype(jnp.bfloat16)

    blocks = query_rows.reshape(
        query_count // block_rows, block_rows, query_rows.shape[1], query_rows.shape[2]
    )
    return lax.map(one_block, blocks).reshape(query_rows.shape)


def regroup_rows(latent_rows, destination, devices):
    tok_rows, features = latent_rows.shape
    capacity = -(-tok_rows // devices)
    target = destination // tok_rows
    dest_pos = destination % tok_rows
    member = (target[:, None] == jnp.arange(devices)[None, :]).astype(jnp.int32)
    before = jnp.sum((jnp.cumsum(member, axis=0) - member) * member, axis=1)
    slot_index = target * capacity + before
    select = jnp.arange(devices * capacity)[:, None] == slot_index[None, :]
    packed = jnp.dot(
        select.astype(jnp.bfloat16), latent_rows, preferred_element_type=jnp.float32
    ).astype(jnp.bfloat16)
    filled = jnp.any(select, axis=1)
    where_to = jnp.where(filled, jnp.sum(jnp.where(select, dest_pos[None, :], 0), axis=1), -1)
    packed = packed.reshape(devices, capacity, features)
    where_to = where_to.reshape(devices, capacity)
    arrived, positions = (
        lax.all_to_all(packed, "seq", split_axis=0, concat_axis=0, tiled=True),
        lax.all_to_all(where_to, "seq", split_axis=0, concat_axis=0, tiled=True),
    )
    picker = (jnp.arange(tok_rows)[:, None] == positions.reshape(1, devices * capacity)).astype(
        jnp.bfloat16
    )
    return jnp.dot(
        picker, arrived.reshape(devices * capacity, features), preferred_element_type=jnp.float32
    ).astype(jnp.bfloat16)


def local(queries, keys, values, destination):
    devices = lax.axis_size("seq")
    tok_rows = queries.shape[0]
    splits = max(1, devices // HEADS)
    per_device = max(1, HEADS // devices)
    part_rows = tok_rows // splits
    head_groups = HEADS // per_device
    shaped = queries.reshape(splits, part_rows, head_groups, per_device, HEAD_DIM)
    query_slots = jnp.transpose(shaped, (1, 2, 0, 3, 4)).reshape(
        part_rows, devices, per_device, HEAD_DIM
    )
    paired_cols = jnp.concatenate(
        (keys.reshape(tok_rows, HEADS, HEAD_DIM), values.reshape(tok_rows, HEADS, HEAD_DIM)), axis=2
    )
    pair_slots = jnp.repeat(
        paired_cols.reshape(tok_rows, head_groups, per_device, 2 * HEAD_DIM), splits, axis=1
    )
    query_heads, pair_heads = (
        lax.all_to_all(query_slots, "seq", split_axis=1, concat_axis=0, tiled=True),
        lax.all_to_all(pair_slots, "seq", split_axis=1, concat_axis=0, tiled=True),
    )
    query_heads = query_heads.reshape(-1, per_device, HEAD_DIM)
    pair_heads = pair_heads.reshape(-1, per_device, 2 * HEAD_DIM)
    attended = attend_local(query_heads, pair_heads[:, :, :HEAD_DIM], pair_heads[:, :, HEAD_DIM:])
    returned = lax.all_to_all(
        attended.reshape(devices, part_rows, per_device, HEAD_DIM),
        "seq",
        split_axis=0,
        concat_axis=0,
        tiled=True,
    )
    returned = returned.reshape(head_groups, splits, part_rows, per_device, HEAD_DIM)
    latent_rows = jnp.transpose(returned, (1, 2, 0, 3, 4)).reshape(tok_rows, HEADS * HEAD_DIM)
    return regroup_rows(latent_rows, destination, devices)


def start_to(me, target, source, landing, send_sem, recv_sem):
    @pl.when(target != me)
    def _():
        pltpu.make_async_remote_copy(
            src_ref=source,
            dst_ref=landing,
            send_sem=send_sem,
            recv_sem=recv_sem,
            device_id={"seq": target},
            device_id_type=pl.DeviceIdType.MESH,
        ).start()

    @pl.when(target == me)
    def _():
        pltpu.make_async_copy(source, landing, recv_sem).start()


def wait_bytes(ref, sem):
    pltpu.make_async_copy(ref, ref, sem).wait()


def attend_kernel(
    devices, heads, q_ref, k_ref, v_ref, spot_ref, out_ref,
    held, spots, spot_row, chosen, moved, weights, totals, mixed,
    spot_send, spot_recv, in_send, in_recv, out_send, out_recv,
):
    me = lax.axis_index("seq")
    rows = q_ref.shape[0]
    tokens = devices * rows
    width = heads * HEAD_DIM
    half = devices // 2
    block = 2 * rows
    factor = math.log2(math.e) / math.sqrt(HEAD_DIM)

    def columns(device, head):
        return pl.ds(pl.multiple_of(device * width + head * HEAD_DIM, LANES), HEAD_DIM)

    def token_rows(device):
        return pl.ds(pl.multiple_of(device * rows, 16), rows)

    barrier = pltpu.get_barrier_semaphore()

    def greet(step, carry):
        pl.semaphore_signal(
            barrier, inc=1, device_id={"seq": lax.rem(me + step, devices)},
            device_id_type=pl.DeviceIdType.MESH,
        )
        return carry

    lax.fori_loop(1, devices, greet, 0, unroll=True)
    pl.semaphore_wait(barrier, devices - 1)

    def send_spots(step, carry):
        target = lax.rem(me + half + step, devices)
        start_to(me, target, spot_ref, spots.at[me], spot_send, spot_recv)
        return carry

    for head in range(heads):
        for kind, whole in enumerate((q_ref, k_ref, v_ref)):

            def send_rows(step, carry):
                target = lax.rem(me + half + step, devices)
                start_to(
                    me, target, whole.at[:, columns(target, head)],
                    held.at[kind, head, token_rows(me)],
                    in_send.at[kind, head], in_recv.at[kind, head],
                )
                return carry

            lax.fori_loop(0, devices, send_rows, 0)
            if head == 0 and kind == 0:
                lax.fori_loop(0, devices, send_spots, 0)

    wait_bytes(spots, spot_recv)
    for device in range(devices):
        spot_row[:, device * rows : (device + 1) * rows] = spots[device]

    def choose(at, carry):
        start = pl.multiple_of(at * block, 16)
        places = lax.broadcasted_iota(jnp.int32, (block, tokens), 0) + start
        chosen[pl.ds(start, block), :] = jnp.where(
            spot_row[...] == places, 1.0, 0.0
        ).astype(jnp.bfloat16)
        return carry

    lax.fori_loop(0, devices // 2, choose, 0)

    for head in range(heads):
        wait_bytes(held.at[0, head], in_recv.at[0, head])

        def move(at, carry):
            here = pl.ds(pl.multiple_of(at * block, 16), block)
            moved[head, here, :] = jnp.dot(
                chosen[here, :], held[0, head], preferred_element_type=jnp.float32
            ).astype(jnp.bfloat16)
            return carry

        lax.fori_loop(0, devices // 2, move, 0)
        wait_bytes(held.at[1, head], in_recv.at[1, head])

        def weigh(at, carry):
            here = pl.ds(pl.multiple_of(at * block, 16), block)
            scores = lax.dot_general(
                moved[head, here, :], held[1, head], (((1,), (1,)), ((), ())),
                preferred_element_type=jnp.float32,
            )
            peak = jnp.max(scores, axis=1, keepdims=True)
            grown = jnp.exp2((scores - peak) * factor)
            totals[here, :] = jnp.sum(grown, axis=1, keepdims=True)
            weights[here, :] = grown.astype(jnp.bfloat16)
            return carry

        lax.fori_loop(0, half, weigh, 0)
        wait_bytes(held.at[2, head], in_recv.at[2, head])

        def attend(step, carry):
            off = half // 2 + ((step + 1) // 2) * (1 - 2 * lax.rem(step, 2))
            at = lax.rem(me // 2 + off, half)
            here = pl.ds(pl.multiple_of(at * block, 16), block)
            result = jnp.dot(
                weights[here, :], held[2, head], preferred_element_type=jnp.float32
            )
            mixed[head, here, :] = (result / totals[here, :]).astype(jnp.bfloat16)
            for one in range(2):
                target = 2 * at + one
                start_to(
                    me, target, mixed.at[head, token_rows(target)],
                    out_ref.at[:, columns(me, head)], out_send, out_recv,
                )
            return carry

        lax.fori_loop(0, half, attend, 0)

    others = pl.ds(0, (devices - 1) * rows)
    wait_bytes(spots.at[pl.ds(0, devices - 1)], spot_send)
    for head in range(heads):
        for kind in range(3):
            wait_bytes(held.at[kind, head, others], in_send.at[kind, head])
    wait_bytes(mixed.at[:, others], out_send)
    wait_bytes(mixed, out_recv)


def local_fused(queries, keys, values, destination):
    devices = lax.axis_size("seq")
    rows = queries.shape[0]
    heads = HEADS // devices
    tokens = devices * rows
    spots = destination.reshape(1, rows)
    large = pl.BlockSpec(memory_space=pltpu.HBM)
    return pl.pallas_call(
        functools.partial(attend_kernel, devices, heads),
        out_shape=jax.ShapeDtypeStruct(queries.shape, jnp.bfloat16),
        in_specs=[large, large, large, pl.BlockSpec(memory_space=pltpu.VMEM)],
        out_specs=pl.BlockSpec(memory_space=pl.ANY),
        scratch_shapes=[
            pltpu.VMEM((3, heads, tokens, HEAD_DIM), jnp.bfloat16),
            pltpu.VMEM((devices, 1, rows), jnp.int32),
            pltpu.VMEM((1, tokens), jnp.int32),
            pltpu.VMEM((tokens, tokens), jnp.bfloat16),
            pltpu.VMEM((heads, tokens, HEAD_DIM), jnp.bfloat16),
            pltpu.VMEM((tokens, tokens), jnp.bfloat16),
            pltpu.VMEM((tokens, 1), jnp.float32),
            pltpu.VMEM((heads, tokens, HEAD_DIM), jnp.bfloat16),
            pltpu.SemaphoreType.DMA,
            pltpu.SemaphoreType.DMA,
            pltpu.SemaphoreType.DMA((3, heads)),
            pltpu.SemaphoreType.DMA((3, heads)),
            pltpu.SemaphoreType.DMA,
            pltpu.SemaphoreType.DMA,
        ],
        compiler_params=pltpu.CompilerParams(
            collective_id=0, has_side_effects=True, vmem_limit_bytes=53 * 2**20
        ),
        name="attend",
    )(queries, keys, values, spots)


def solution(mesh):
    devices = mesh.shape["seq"]
    fused = HEADS % devices == 0 and devices % 4 == 0
    return jax.shard_map(
        local_fused if fused else local,
        mesh=mesh,
        in_specs=(
            P(("group", "seq"), None),
            P(("group", "seq"), None),
            P(("group", "seq"), None),
            P(("group", "seq")),
        ),
        out_specs=P(("group", "seq"), None),
        check_vma=False,
    )
```
